256 devices in a mesh: fsdp: 8 (over x, core), tp: 32 (over y, z).
Axes of the slice: x: 4, y: 4, z: 8, core: 2. Of those that a mesh axis runs over, the one named last changes fastest.
Arguments:
- momentum: float32 [8192, 28672], P('fsdp', 'tp'), may hold values from -6 to 6
- gradient: bfloat16 [8192, 28672], P('fsdp', 'tp'), may hold values from -6 to 6
- right_factor: float32 [512, 28672], P('fsdp', 'tp'), may hold values from -0.03125 to 0.03125
Outputs:
- new_momentum: float32 [8192, 28672], P('fsdp', 'tp')
- update: bfloat16 [8192, 28672], P('fsdp', 'tp')
- new_factor: float32 [512, 28672], P('fsdp', 'tp')
The draws below stay inside these ranges and needn't reach their ends.
All inputs are finite; a program needn't handle non-finite values.
Results may differ from the reference program's by a relative error of at most 0.001.
Values sent between devices are 32-bit elements; how exact they have to be, the bound alone decides.
No kernel may reach another device: no remote copies, remote signals or barrier semaphores. Data moves between devices by JAX's collectives and lax.ppermute only.
A program may use at most 64 MiB of HBM per device.

```python
import math
import jax
import jax.numpy as jnp
from jax import lax

D = 8192
FF = 28672
RANK = 512


def steps_of(own_key, dims, pieces, low, high):
    def one(position, shards_of):
        draws = jax.random.uniform(jax.random.fold_in(jax.random.fold_in(own_key, 6), position), (shards_of,), jnp.float32, low / len(pieces), high / len(pieces))
        return jnp.repeat(jnp.exp(draws), dims[position] // shards_of).reshape((-1,) + (1,) * (len(dims) - position - 1))

    gain = one(*pieces[0])
    for cut in pieces[1:]:
        gain = gain * one(*cut)
    return gain


def scatter_about(key, extent, width, reach, split=(), held_as=jnp.bfloat16):
    array = width * jax.random.normal(key, extent, jnp.float32)
    if split:
        array = array * steps_of(key, extent, split, -0.22, 0.18)
    return jnp.clip(array, -reach, reach).astype(held_as)


def setup_inputs(seed: int = 0) -> dict:
    key_of = jax.random.split(jax.random.key(seed), 4)
    momentum = scatter_about(key_of[0], (D, FF), 1.0, 6.0, ((0, 8), (1, 32)), jnp.float32)
    gradient = scatter_about(key_of[1], (D, FF), 1.0, 6.0, ((0, 8), (1, 32)))
    right_factor = scatter_about(key_of[2], (RANK, FF), FF ** -0.5, 0.03125, ((0, 8), (1, 32)), jnp.float32)
    return {"momentum": momentum, "gradient": gradient, "right_factor": right_factor}


decay_rest = 0.05
epsilon = 1e-06

def product(left, right):
    return jnp.dot(left.astype(jnp.float32), right.astype(jnp.float32), precision=lax.Precision.HIGHEST, preferred_element_type=jnp.float32)

def reference(momentum, gradient, right_factor):
    combined = momentum + gradient.astype(jnp.float32)
    left = product(combined, right_factor.T)
    gram = product(left.T, left)
    lower = jnp.linalg.cholesky(gram)
    orth = jax.scipy.linalg.solve_triangular(lower, left.T, lower=True).T
    right = product(orth.T, combined)
    norms = jnp.sqrt(lax.optimization_barrier(jnp.sum(right * right, axis=1, keepdims=True)) + epsilon)
    new_factor = right / norms
    new_momentum = combined - decay_rest * product(orth, right)
    scale_rms = math.sqrt(D * FF / RANK)
    update = (scale_rms * product(orth, new_factor)).astype(jnp.bfloat16)
    return (new_momentum, update, new_factor)
```

```python
import math

import jax
import jax.numpy as jnp
from jax import lax
from jax.experimental import pallas as pl
from jax.experimental.pallas import tpu as pltpu
from jax.sharding import Mesh
from jax.sharding import PartitionSpec as P

D = 8192
FF = 28672
RANK = 512

decay_rest = 0.05
epsilon = 1e-06

SIZES = {"x": 4, "c": 2, "y": 4, "z": 8}
ROWS = ("x", "c")
COLS = ("y", "z")

CLOSE = 2e-3
MOST_STEPS = 9

HIGH = lax.Precision.HIGH


def dot(a, b, contract=(1, 0), precision=HIGH):
    return lax.dot_general(
        a, b, (((contract[0],), (contract[1],)), ((), ())), precision=precision, preferred_element_type=jnp.float32
    )


def shift(a, axis, k):
    n = SIZES[axis]
    return lax.ppermute(a, axis, [(i, (i + k) % n) for i in range(n)])


def block_of(a, index, rows):
    return lax.dynamic_slice_in_dim(a, index * rows, rows, 0)


def placed(blocks, indices):
    rows, columns = blocks[0].shape
    out = jnp.zeros((rows * len(blocks), columns), jnp.float32)
    for block, index in zip(blocks, indices):
        out = lax.dynamic_update_slice_in_dim(out, block, index * rows, 0)
    return out


def scatter_sum(part, axis):
    n, me = SIZES[axis], lax.axis_index(axis)
    arrived = [shift(part((me + k) % n), axis, k) for k in range(1, n)]
    total = part(me)
    for a in arrived:
        total = total + a
    return total


def gathered(a, axis):
    n, me = SIZES[axis], lax.axis_index(axis)
    arrived = [shift(a, axis, k) for k in range(1, n)]
    return placed([a] + arrived, [me] + [(me - k) % n for k in range(1, n)])


def scatter_sum_z(a):
    n = SIZES["z"]
    swapped = lax.all_to_all(a, "z", split_axis=0, concat_axis=0, tiled=True)
    return jnp.sum(swapped.reshape((n, a.shape[0] // n, a.shape[1])), axis=0)


def gathered_z(a):
    n = SIZES["z"]
    many = jnp.broadcast_to(a[None], (n,) + a.shape).reshape((n * a.shape[0], a.shape[1]))
    return lax.all_to_all(many, "z", split_axis=0, concat_axis=0, tiled=True)


def sum_over_rows(a):
    half, eighth = a.shape[0] // 2, a.shape[0] // 8
    c = lax.axis_index("c")
    mine = block_of(a, c, half) + shift(block_of(a, 1 - c, half), "c", 1)
    own = scatter_sum(lambda i: block_of(mine, i, eighth), "x")
    return gathered(gathered(own, "x"), "c")


def gathered_factor(a):
    c = lax.axis_index("c")
    mine = gathered(a, "x").reshape((SIZES["x"], 1) + a.shape)
    other = shift(mine, "c", 1)
    out = jnp.zeros((SIZES["x"], 2) + a.shape, jnp.float32)
    out = lax.dynamic_update_slice_in_dim(out, mine, c, 1)
    out = lax.dynamic_update_slice_in_dim(out, other, 1 - c, 1)
    return out.reshape((8 * a.shape[0], a.shape[1]))


def split(a):
    high = a.astype(jnp.bfloat16)
    return high, (a - high.astype(jnp.float32)).astype(jnp.bfloat16)


def dot3(a, b, contract=(1, 0)):
    (ah, al), (bh, bl) = a, b
    dims = (((contract[0],), (contract[1],)), ((), ()))

    def one(p, q):
        return lax.dot_general(p, q, dims, preferred_element_type=jnp.float32)

    return one(ah, bh) + (one(ah, bl) + one(al, bh))


def newton_kernel(gram_ref, inverse_ref, residual_ref, scaled_ref, w_ref):
    n = gram_ref.shape[0]
    row = lax.broadcasted_iota(jnp.int32, (n, n), 0)
    column = lax.broadcasted_iota(jnp.int32, (n, n), 1)
    eye = (row == column).astype(jnp.float32)
    keep = jnp.where(row > column, 1.0, 0.5 * eye)
    gram = gram_ref[...]
    diagonal = gram * eye
    by_row = lax.rsqrt(jnp.sum(diagonal, axis=1, keepdims=True))
    by_column = lax.rsqrt(jnp.sum(diagonal, axis=0, keepdims=True))
    scaled = gram * by_row * by_column
    scaled_ref[...] = scaled
    w_ref[...] = eye - (scaled - eye) * keep

    def more(state):
        step, residual = state
        return jnp.logical_and(step < MOST_STEPS, jnp.logical_not(residual < CLOSE))

    def update(state):
        step, _ = state
        w = split(w_ref[...])
        error = dot3(split(dot3(w, split(scaled_ref[...]))), w, (1, 1)) - eye
        w_ref[...] = w_ref[...] - dot3(split(error * keep), w)
        return step + 1, jnp.sqrt(jnp.sum(error * error))

    _, residual = lax.while_loop(more, update, (jnp.int32(0), jnp.float32(1.0)))
    inverse_ref[...] = w_ref[...] * by_column
    residual_ref[0, 0] = residual


def directly(gram, _):
    lower = jnp.linalg.cholesky(gram)
    return jax.scipy.linalg.solve_triangular(lower, jnp.eye(gram.shape[0], dtype=jnp.float32), lower=True)


def inverse_factor(gram):
    n = gram.shape[0]
    inverse, residual = pl.pallas_call(
        newton_kernel,
        out_shape=(jax.ShapeDtypeStruct((n, n), jnp.float32), jax.ShapeDtypeStruct((1, 1), jnp.float32)),
        in_specs=[pl.BlockSpec(memory_space=pltpu.VMEM)],
        out_specs=(pl.BlockSpec(memory_space=pltpu.VMEM), pl.BlockSpec(memory_space=pltpu.SMEM)),
        scratch_shapes=[pltpu.VMEM((n, n), jnp.float32)] * 2,
        compiler_params=pltpu.CompilerParams(vmem_limit_bytes=32 * 2**20),
    )(gram)
    return lax.cond(residual[0, 0] < CLOSE, lambda _, w: w, directly, gram, inverse)


def per_device(momentum, gradient, right_factor):
    y = lax.axis_index("y")
    combined = momentum + gradient.astype(jnp.float32)
    whole_factor = gathered_factor(right_factor)
    rows = combined.shape[0] // SIZES["y"]
    band = scatter_sum(lambda i: dot(block_of(combined, i, rows), whole_factor, (1, 1)), "y")
    band = gathered_z(scatter_sum_z(band))
    left = gathered(band, "y")
    gram = sum_over_rows(dot(left, left, (0, 0)))
    crossed = sum_over_rows(dot(left, combined, (0, 0)))
    inverse = inverse_factor(gram)
    orth = dot(left, inverse, (1, 1))
    right = dot(inverse, crossed)
    squared = jnp.sum(right * right, axis=1).reshape((4, 128))
    copies = jnp.broadcast_to(squared[None], (32, 4, 128)).reshape((128, 128))
    squared = jnp.sum(
        lax.all_to_all(copies, COLS, split_axis=0, concat_axis=0, tiled=True).reshape((32, 4, 128)), axis=0
    ).reshape((RANK,))
    factor_full = right / jnp.sqrt(squared + epsilon)[:, None]
    block = right_factor.shape[0]
    new_factor = block_of(factor_full, lax.axis_index("x") * 2 + lax.axis_index("c"), block)
    new_momentum = combined - decay_rest * dot(orth, right, precision=lax.Precision.DEFAULT)
    update = (math.sqrt(D * FF / RANK) * dot(orth, factor_full)).astype(jnp.bfloat16)
    return (new_momentum, update, new_factor)


def solution(mesh):
    split_mesh = Mesh(mesh.devices.reshape(tuple(SIZES.values())), tuple(SIZES))
    spec = P(ROWS, COLS)
    return jax.shard_map(
        per_device, mesh=split_mesh, in_specs=(spec, spec, spec), out_specs=(spec, spec, spec), check_vma=False
    )
```

```python
import functools
import math

import jax
import jax.numpy as jnp
from jax import lax
from jax.experimental import pallas as pl
from jax.experimental.pallas import tpu as pltpu
from jax.sharding import Mesh
from jax.sharding import PartitionSpec as P

D = 8192
FF = 28672
RANK = 512

decay_rest = 0.05
epsilon = 1e-06

SIZES = {"x": 4, "c": 2, "y": 4, "z": 8}
ROWS = ("x", "c")
COLS = ("y", "z")

CLOSE = 5e-3
MOST_STEPS = 9

TILE = 128


def shift(a, axis, k):
    n = SIZES[axis]
    return lax.ppermute(a, axis, [(i, (i + k) % n) for i in range(n)])


def block_of(a, index, rows):
    return lax.dynamic_slice_in_dim(a, index * rows, rows, 0)


def summed_z(a):
    spread = call(spread_kernel, (exchange(a, "z"),), f32(*a.shape), [], name="spread")
    return exchange(spread, "z")


def exchange(a, axes):
    return lax.all_to_all(a, axes, split_axis=0, concat_axis=0, tiled=True)


def relative(a, axis):
    return [a] + [shift(a, axis, k) for k in range(1, SIZES[axis])]


def split(a):
    high = a.astype(jnp.bfloat16)
    return high, (a - high.astype(jnp.float32)).astype(jnp.bfloat16)


def dot3(a, b, contract=(1, 0)):
    (ah, al), (bh, bl) = a, b
    dims = (((contract[0],), (contract[1],)), ((), ()))
    n = ah.shape[0]
    both = lax.dot_general(jnp.concatenate([ah, al]), bh, dims, preferred_element_type=jnp.float32)
    return both[:n] + (both[n:] + lax.dot_general(ah, bl, dims, preferred_element_type=jnp.float32))


def dot1(a, b, contract=(1, 0)):
    return lax.dot_general(
        a[0], b[0], (((contract[0],), (contract[1],)), ((), ())), preferred_element_type=jnp.float32
    )


def spread_kernel(parts_ref, out_ref):
    rows = parts_ref.shape[0] // SIZES["z"]
    total = parts_ref[:rows]
    for i in range(1, SIZES["z"]):
        total = total + parts_ref[i * rows : (i + 1) * rows]
    for i in range(SIZES["z"]):
        out_ref[i * rows : (i + 1) * rows] = total


def join_kernel(*refs):
    parts, out_ref = refs[:-1], refs[-1]
    n = parts[0].shape[0]
    out_ref[:n] = parts[0][...] + parts[1][...] + parts[2][...]
    out_ref[n:] = parts[3][...] + parts[4][...] + parts[5][...]


def combine_kernel(momentum_ref, gradient_ref, high_ref, low_ref):
    high_ref[...], low_ref[...] = split(momentum_ref[...] + gradient_ref[...].astype(jnp.float32))


def left_kernel(order_ref, y_ref, *refs):
    blocks, (high_ref, low_ref), outs, (factor_ref, left_ref) = refs[:8], refs[8:10], refs[10:18], refs[18:]
    rows = blocks[0].shape[0]
    for i, block in enumerate(blocks):
        factor_ref[pl.ds(pl.multiple_of(order_ref[i] * rows, rows), rows)] = block[...]
    factor = split(factor_ref[...].T)
    n = outs[0].shape[0]
    for i in range(4):
        at = slice(2 * i * n, 2 * (i + 1) * n)
        left_ref[at] = dot3((high_ref[at], low_ref[at]), factor)
    for k, out in enumerate(outs):
        out[...] = left_ref[pl.ds(pl.multiple_of(lax.rem(2 * y_ref[0] + k, 8) * n, n), n)]


def gram_kernel(band_ref, packed_ref):
    band = band_ref[...]
    across, down = split(band.T), split(band)
    at = 0
    for i in range(RANK // TILE):
        product = dot3(
            tuple(p[i * TILE : (i + 1) * TILE] for p in across), tuple(p[:, : (i + 1) * TILE] for p in down)
        )
        for j in range(i + 1):
            packed_ref[at : at + TILE] = product[:, j * TILE : (j + 1) * TILE]
            at += TILE


def absorb_kernel(places, accumulate, place_ref, *refs):
    n = len(places)
    bands, (high_ref, low_ref), refs = refs[:n], refs[n : n + 2], refs[n + 2 :]
    before, halves = (refs[:2], refs[2:]) if accumulate else (None, refs)
    c, y = place_ref[0], place_ref[1]
    h, own = RANK // 2, RANK // 8
    tiles = high_ref.shape[1] // TILE
    for p, half in enumerate(halves):
        core = 1 - c if p == 0 else c
        total = None
        for band_ref, (k, first) in zip(bands, places):
            ranks = split(band_ref[:, pl.ds(pl.multiple_of(core * h, h), h)].T)
            start = lax.rem(y + 4 - k, 4) * (high_ref.shape[0] // 4) + first
            rows = pl.ds(pl.multiple_of(start, TILE), band_ref.shape[0])
            term = dot3(ranks, (high_ref[rows], low_ref[rows]))
            total = term if total is None else total + term
        for i in range(4):
            for j in range(tiles):
                at = (i * tiles + j) * own
                piece = total[i * own : (i + 1) * own, j * TILE : (j + 1) * TILE]
                half[at : at + own] = piece + before[p][at : at + own] if accumulate else piece


def settle_kernel(*refs):
    total = refs[0][...]
    for a in refs[1:-1]:
        total = total + a[...]
    refs[-1][...] = total


def unpack(packed_ref, gram_ref):
    at = 0
    for i in range(RANK // TILE):
        for j in range(i + 1):
            block = packed_ref[at : at + TILE]
            rows, columns = slice(i * TILE, (i + 1) * TILE), slice(j * TILE, (j + 1) * TILE)
            gram_ref[rows, columns] = block
            if i != j:
                gram_ref[columns, rows] = block.T
            at += TILE


def eliminate(gram_ref, inverse_ref):
    n = gram_ref.shape[0]
    row = lax.broadcasted_iota(jnp.int32, (n, n), 0)
    column = lax.broadcasted_iota(jnp.int32, (n, n), 1)
    inverse_ref[...] = (row == column).astype(jnp.float32)

    def step(j, _):
        gram, inverse = gram_ref[...], inverse_ref[...]
        below = lax.broadcasted_iota(jnp.int32, (n, 1), 0)
        pivot_row = jnp.sum(jnp.where(row == j, gram, 0.0), axis=0, keepdims=True)
        pivot_inverse = jnp.sum(jnp.where(row == j, inverse, 0.0), axis=0, keepdims=True)
        pivot = jnp.sum(jnp.where(column[:1] == j, pivot_row, 0.0), axis=1, keepdims=True)
        scale = 1.0 / jnp.sqrt(pivot)
        factor = jnp.sum(jnp.where(column == j, gram, 0.0), axis=1, keepdims=True) * scale
        factor = jnp.where(below > j, factor, 0.0)
        gram_ref[...] = gram - factor * (pivot_row * scale)
        inverse = inverse - factor * (pivot_inverse * scale)
        inverse_ref[...] = jnp.where(row == j, pivot_inverse * scale, inverse)
        return 0

    lax.fori_loop(0, n, step, 0)


def inverse_factor_kernel(order_ref, *refs):
    blocks, (inverse_ref, packed_ref, gram_ref, w_ref) = refs[:8], refs[8:]
    n, h = RANK, RANK // 2
    rows = blocks[0].shape[0]
    for i, block in enumerate(blocks):
        packed_ref[pl.ds(pl.multiple_of(order_ref[i] * rows, 8), rows)] = block[...]
    unpack(packed_ref, gram_ref)
    row = lax.broadcasted_iota(jnp.int32, (n, n), 0)
    column = lax.broadcasted_iota(jnp.int32, (n, n), 1)
    eye = (row == column).astype(jnp.float32)
    keep = jnp.where(row > column, 1.0, 0.5 * eye)
    gram = gram_ref[...]
    diagonal = gram * eye
    by_row = lax.rsqrt(jnp.sum(diagonal, axis=1, keepdims=True))
    by_column = lax.rsqrt(jnp.sum(diagonal, axis=0, keepdims=True))
    scaled = gram * by_row * by_column
    w_ref[...] = eye - (scaled - eye) * keep
    top, low = split(scaled)
    a11, a12, a21, a22 = (
        (top[r, c], low[r, c]) for r in (slice(0, h), slice(h, n)) for c in (slice(0, h), slice(h, n))
    )
    eye_h, keep_h = eye[:h, :h], keep[:h, :h]

    def more(state):
        step, residual = state
        return jnp.logical_and(step < MOST_STEPS, jnp.logical_not(residual < CLOSE))

    def update(state, product=dot3):
        step, _ = state
        w11, w21, w22 = split(w_ref[:h, :h]), split(w_ref[h:, :h]), split(w_ref[h:, h:])
        t11 = split(product(w11, a11))
        t21 = split(product(w21, a11) + product(w22, a21))
        t22 = split(product(w21, a12) + product(w22, a22))
        e11 = product(t11, w11, (1, 1)) - eye_h
        e21 = product(t21, w11, (1, 1))
        e22 = product(t21, w21, (1, 1)) + product(t22, w22, (1, 1)) - eye_h
        p11, p21, p22 = split(e11 * keep_h), split(e21), split(e22 * keep_h)
        w_ref[:h, :h] = w_ref[:h, :h] - dot1(p11, w11)
        w_ref[h:, :h] = w_ref[h:, :h] - (dot1(p21, w11) + dot1(p22, w21))
        w_ref[h:, h:] = w_ref[h:, h:] - dot1(p22, w22)
        return step + 1, jnp.sqrt(jnp.sum(e11 * e11) + 2.0 * jnp.sum(e21 * e21) + jnp.sum(e22 * e22))

    start = update((jnp.int32(0), None), dot1)
    _, residual = lax.while_loop(more, update, (start[0], jnp.float32(1.0)))
    inverse_ref[...] = w_ref[...] * by_column

    @pl.when(jnp.logical_not(residual < CLOSE))
    def _():
        eliminate(gram_ref, inverse_ref)


def orth_kernel(y_ref, inverse_ref, *refs):
    bands, out_ref = refs[:-1], refs[-1]
    inverse = split(inverse_ref[...])
    n = out_ref.shape[0] // 4
    for band, (k, first) in zip(bands, ((0, 0), (1, 0), (2, 0), (2, n // 2), (3, 0))):
        at = pl.ds(pl.multiple_of(lax.rem(y_ref[0] + 4 - k, 4) * n + first, TILE), band.shape[0])
        out_ref[at] = dot3(split(band[...]), inverse, (1, 1))


def right_kernel(order_ref, *refs):
    blocks, (inverse_ref, right_ref, squared_ref, crossed_ref) = refs[:8], refs[8:]
    rows, h = RANK // 8, RANK // 2
    for i, block in enumerate(blocks):
        at = pl.ds(pl.multiple_of(order_ref[i] * rows, rows), rows)
        for j in range(right_ref.shape[1] // TILE):
            crossed_ref[at, j * TILE : (j + 1) * TILE] = block[j * rows : (j + 1) * rows]
    crossed = split(crossed_ref[...])
    inverse = split(inverse_ref[...])
    right_ref[:h] = dot3(tuple(p[:h, :h] for p in inverse), tuple(p[:h] for p in crossed))
    right_ref[h:] = dot3(tuple(p[h:] for p in inverse), crossed)
    right = right_ref[...]
    total = right[:, :TILE] * right[:, :TILE]
    for j in range(1, right.shape[1] // TILE):
        piece = right[:, j * TILE : (j + 1) * TILE]
        total = total + piece * piece
    sums = jnp.sum(total.T, axis=0, keepdims=True)
    for i in range(RANK // TILE):
        squared_ref[:, i, :] = jnp.broadcast_to(sums[:, i * TILE : (i + 1) * TILE], (squared_ref.shape[0], TILE))


def momentum_kernel(momentum_ref, gradient_ref, orth_ref, right_ref, out_ref, right_low):
    @pl.when(pl.program_id(0) == 0)
    def _():
        right_low[...] = right_ref[...].astype(jnp.bfloat16)

    product = jnp.dot(orth_ref[...].astype(jnp.bfloat16), right_low[...], preferred_element_type=jnp.float32)
    out_ref[...] = (momentum_ref[...] + gradient_ref[...].astype(jnp.float32)) - decay_rest * product


def update_kernel(place_ref, squared_ref, orth_ref, right_ref, update_ref, factor_ref, split_ref):
    squared = jnp.sum(squared_ref[...], axis=0)
    over = 1.0 / jnp.sqrt(squared + epsilon)
    over = jnp.concatenate([over[i : i + 1] for i in range(RANK // TILE)], axis=1)

    @pl.when(pl.program_id(0) == 0)
    def _():
        split_ref[0], split_ref[1] = split(right_ref[...])
        rows = factor_ref.shape[0]
        at = pl.multiple_of(place_ref[0] * rows, 8)
        row = lax.broadcasted_iota(jnp.int32, (rows, RANK), 0)
        column = lax.broadcasted_iota(jnp.int32, (rows, RANK), 1)
        own = jnp.sum(jnp.where(column == row + at, jnp.broadcast_to(over, (rows, RANK)), 0.0), axis=1, keepdims=True)
        factor_ref[...] = right_ref[pl.ds(at, rows)] * own

    orth = split(orth_ref[...] * over)
    update_ref[...] = (math.sqrt(D * FF / RANK) * dot3(orth, (split_ref[0], split_ref[1]))).astype(jnp.bfloat16)


def in_hbm(a):
    return pltpu.with_memory_space_constraint(a, pltpu.HBM)


def in_vmem(a):
    return pltpu.with_memory_space_constraint(a, pltpu.VMEM)


VMEM_BYTES = 20 * 2**20
VMEM, SMEM = pl.BlockSpec(memory_space=pltpu.VMEM), pl.BlockSpec(memory_space=pltpu.SMEM)


def call(kernel, given, out, scratch=(), name=None, flops=10**9):
    return pl.pallas_call(
        kernel,
        out_shape=out,
        in_specs=[SMEM if a.dtype == jnp.int32 else VMEM for a in given],
        out_specs=jax.tree.map(lambda _: VMEM, out),
        scratch_shapes=list(scratch),
        compiler_params=pltpu.CompilerParams(vmem_limit_bytes=VMEM_BYTES),
        cost_estimate=pl.CostEstimate(flops=flops, bytes_accessed=2**22, transcendentals=0),
        name=name,
    )(*given)


def f32(*shape):
    return jax.ShapeDtypeStruct(shape, jnp.float32)


def by_rows(kernel, given, out, scratch=(), name=None, flops=10**9):
    n = D // 8

    def spec(a):
        if a.shape[0] == n:
            return pl.BlockSpec((n // 4, a.shape[1]), lambda i: (i, 0))
        if a.dtype == jnp.int32:
            return SMEM
        return pl.BlockSpec(a.shape, lambda i: (0,) * len(a.shape))

    return pl.pallas_call(
        kernel,
        grid=(4,),
        out_shape=out,
        in_specs=[spec(a) for a in given],
        out_specs=jax.tree.map(spec, out),
        scratch_shapes=list(scratch),
        compiler_params=pltpu.CompilerParams(vmem_limit_bytes=VMEM_BYTES),
        cost_estimate=pl.CostEstimate(flops=flops, bytes_accessed=2**23, transcendentals=0),
        name=name,
    )(*given)


def per_device(momentum, gradient, right_factor):
    x, c, y = lax.axis_index("x"), lax.axis_index("c"), lax.axis_index("y")
    rows, columns = momentum.shape[0] // SIZES["y"], momentum.shape[1]
    wide = jax.ShapeDtypeStruct(momentum.shape, jnp.bfloat16)
    combined = by_rows(combine_kernel, (momentum, gradient), (wide, wide), name="combine")

    factor = relative(right_factor, "x")
    factor, combined = lax.optimization_barrier((factor, combined))
    factor = factor + [shift(b, "c", 1) for b in factor]
    order = jnp.stack([((x - k) % 4) * 2 + p for p in (c, 1 - c) for k in range(4)])
    terms = call(
        left_kernel,
        (order, y[None], *factor, *map(in_vmem, combined)),
        [f32(rows // 2, RANK)] * 8,
        [pltpu.VMEM((RANK, columns), jnp.float32), pltpu.VMEM((4 * rows, RANK), jnp.float32)],
        "left",
    )
    by_next, by_last = shift(terms[4], "y", 1), shift(terms[5], "y", 3)
    plain = shift(terms[3], "y", 1), shift(terms[6], "y", 3)
    passed = shift(terms[2] + by_next, "y", 1), shift(terms[7] + by_last, "y", 3)
    band = call(
        join_kernel, (terms[0], passed[0], plain[1], terms[1], plain[0], passed[1]), f32(rows, RANK), name="join"
    )
    band = summed_z(band)
    behind, ahead = shift(band, "y", 1), shift(band, "y", 3)
    across = shift(ahead[: rows // 2], "y", 3), shift(behind[rows // 2 :], "y", 1)

    place = jnp.stack([c, y])
    own, eighth = RANK // 8 * (columns // TILE), 10 * TILE // 8
    packed_rows, half = f32(10 * TILE, TILE), f32(4 * own, TILE)
    packed = call(gram_kernel, (band,), packed_rows, name="gram")

    def absorb(name, pieces, before):
        return call(
            functools.partial(absorb_kernel, [p[1:] for p in pieces], before is not None),
            (place, *[p[0] for p in pieces], *map(in_vmem, combined), *(before or ())),
            (half, half),
            name="absorb_" + name,
        )

    def exchanged(sent, kept):
        n = sent.shape[0] // 4
        came = shift(sent, "c", 1)
        return [block_of(came, (x + k) % 4, n) + block_of(kept, (x + k) % 4, n) for k in range(4)]

    def settled(parts, name):
        terms = [parts[0]] + [shift(parts[k], "x", k) for k in range(1, 4)]
        return call(settle_kernel, terms, f32(*parts[0].shape), name="settle_" + name)

    own_band, packed = lax.optimization_barrier((band, packed))
    halves = absorb("own", ((own_band, 0, 0),), None)
    parts = exchanged(block_of(packed, 1 - c, 4 * eighth), block_of(packed, c, 4 * eighth))
    parts, halves = lax.optimization_barrier((parts, halves))
    halves = absorb("near", ((behind, 1, 0), (ahead, 3, 0)), halves)
    packed = settled(parts, "gram")
    packed = call(settle_kernel, relative(packed, "y"), f32(eighth, TILE), name="settle_gram_y")
    packed, halves = lax.optimization_barrier((packed, halves))
    halves = absorb("far", ((across[0], 2, 0), (across[1], 2, rows // 2)), halves)
    packed = relative(packed, "x")
    parts = exchanged(*halves)
    parts, packed = lax.optimization_barrier((parts, packed))
    packed = packed + [shift(b, "c", 1) for b in packed]
    order = jnp.stack([p * 4 + (x - k) % 4 for p in (c, 1 - c) for k in range(4)])
    inverse = call(
        inverse_factor_kernel,
        (order, *packed),
        f32(RANK, RANK),
        [pltpu.VMEM((10 * TILE, TILE), jnp.float32)] + [pltpu.VMEM((RANK, RANK), jnp.float32)] * 2,
        name="inverse_factor",
    )
    terms = [parts[0]] + [shift(parts[k], "x", k) for k in range(1, 4)]
    terms, inverse = lax.optimization_barrier((terms, inverse))
    crossed = relative(call(settle_kernel, terms, f32(own, TILE), name="settle_crossed"), "x")
    orth = call(orth_kernel, (y[None], inverse, band, behind, *across, ahead), f32(momentum.shape[0], RANK), name="orth")
    crossed, orth = lax.optimization_barrier((crossed, orth))
    crossed = crossed + [shift(b, "c", 1) for b in crossed]
    right, squared = call(
        right_kernel,
        (order, *crossed, inverse),
        (f32(RANK, columns), f32(32, RANK // TILE, TILE)),
        [pltpu.VMEM((RANK, columns), jnp.float32)],
        "right",
    )
    right = in_hbm(right)
    squared = exchange(squared, COLS)
    new_momentum = by_rows(
        momentum_kernel,
        (in_hbm(momentum), in_hbm(gradient), orth, right),
        f32(*momentum.shape),
        [pltpu.VMEM((RANK, columns), jnp.bfloat16)],
        "momentum",
    )
    squared, new_momentum = lax.optimization_barrier((squared, new_momentum))
    update, new_factor = by_rows(
        update_kernel,
        ((x * 2 + c)[None], squared, orth, right),
        (wide, f32(*right_factor.shape)),
        [pltpu.VMEM((2, RANK, columns), jnp.bfloat16)],
        "update",
    )
    return (new_momentum, update, new_factor)


def solution(mesh):
    split_mesh = Mesh(mesh.devices.reshape(tuple(SIZES.values())), tuple(SIZES))
    spec = P(ROWS, COLS)
    return jax.shard_map(
        per_device, mesh=split_mesh, in_specs=(spec, spec, spec), out_specs=(spec, spec, spec), check_vma=False
    )
```

```python
import functools
import math

import jax
import jax.numpy as jnp
from jax import lax
from jax.experimental import pallas as pl
from jax.experimental.pallas import tpu as pltpu
from jax.sharding import Mesh
from jax.sharding import PartitionSpec as P

D = 8192
FF = 28672
RANK = 512

decay_rest = 0.05
epsilon = 1e-06

SIZES = {"x": 4, "c": 2, "y": 4, "z": 8}
ROWS = ("x", "c")
COLS = ("y", "z")

CLOSE = 5e-3
MOST_STEPS = 9

TILE = 128


def shift(a, axis, k):
    n = SIZES[axis]
    return lax.ppermute(a, axis, [(i, (i + k) % n) for i in range(n)])


def block_of(a, index, rows):
    return lax.dynamic_slice_in_dim(a, index * rows, rows, 0)


def summed_z(a):
    spread = call(spread_kernel, (exchange(a, "z"),), f32(*a.shape), [], name="spread")
    return exchange(spread, "z")


def exchange(a, axes):
    return lax.all_to_all(a, axes, split_axis=0, concat_axis=0, tiled=True)


def relative(a, axis):
    return [a] + [shift(a, axis, k) for k in range(1, SIZES[axis])]


def split(a):
    high = a.astype(jnp.bfloat16)
    return high, (a - high.astype(jnp.float32)).astype(jnp.bfloat16)


def dot3(a, b, contract=(1, 0)):
    (ah, al), (bh, bl) = a, b
    dims = (((contract[0],), (contract[1],)), ((), ()))
    n = ah.shape[0]
    both = lax.dot_general(jnp.concatenate([ah, al]), bh, dims, preferred_element_type=jnp.float32)
    return both[:n] + (both[n:] + lax.dot_general(ah, bl, dims, preferred_element_type=jnp.float32))


def dot1(a, b, contract=(1, 0)):
    return lax.dot_general(
        a[0], b[0], (((contract[0],), (contract[1],)), ((), ())), preferred_element_type=jnp.float32
    )


def spread_kernel(parts_ref, out_ref):
    rows = parts_ref.shape[0] // SIZES["z"]
    total = parts_ref[:rows]
    for i in range(1, SIZES["z"]):
        total = total + parts_ref[i * rows : (i + 1) * rows]
    for i in range(SIZES["z"]):
        out_ref[i * rows : (i + 1) * rows] = total


def join_kernel(*refs):
    parts, out_ref = refs[:-1], refs[-1]
    n = parts[0].shape[0]
    out_ref[:n] = parts[0][...] + parts[1][...] + parts[2][...]
    out_ref[n:] = parts[3][...] + parts[4][...] + parts[5][...]


def combine_kernel(momentum_ref, gradient_ref, high_ref, low_ref):
    high_ref[...], low_ref[...] = split(momentum_ref[...] + gradient_ref[...].astype(jnp.float32))


def left_kernel(order_ref, y_ref, *refs):
    blocks, (high_ref, low_ref), outs, (factor_ref, left_ref) = refs[:8], refs[8:10], refs[10:18], refs[18:]
    rows = blocks[0].shape[0]
    for i, block in enumerate(blocks):
        factor_ref[pl.ds(pl.multiple_of(order_ref[i] * rows, rows), rows)] = block[...]
    factor = split(factor_ref[...].T)
    n = outs[0].shape[0]
    for i in range(4):
        at = slice(2 * i * n, 2 * (i + 1) * n)
        left_ref[at] = dot3((high_ref[at], low_ref[at]), factor)
    for k, out in enumerate(outs):
        out[...] = left_ref[pl.ds(pl.multiple_of(lax.rem(2 * y_ref[0] + k, 8) * n, n), n)]


def absorb_kernel(shifts, accumulate, place_ref, *refs):
    bands = []
    for k in shifts:
        n = 2 if k else 1
        bands, refs = bands + [refs[:n]], refs[n:]
    (high_ref, low_ref), refs = refs[:2], refs[2:]
    before, refs = (refs[:2], refs[2:]) if accumulate else (None, refs)
    halves, (packed_ref,) = refs[:2], refs[2:]
    c, y = place_ref[0], place_ref[1]
    h, own, eighth = RANK // 2, RANK // 8, packed_ref.shape[0] // 8
    tiles = high_ref.shape[1] // TILE
    block = halves[0].shape[0] // 4
    grams = [None] * (RANK // TILE)
    for pieces in bands:
        band = jnp.concatenate([p[...] for p in pieces])
        across, down = split(band.T), split(band)
        for i in range(RANK // TILE):
            product = dot3(
                tuple(p[i * TILE : (i + 1) * TILE] for p in across), tuple(p[:, : (i + 1) * TILE] for p in down)
            )
            grams[i] = product if grams[i] is None else grams[i] + product
    at = 0
    for i, product in enumerate(grams):
        for j in range(i + 1):
            packed_ref[at : at + TILE] = product[:, j * TILE : (j + 1) * TILE]
            at += TILE
    for p, half in enumerate(halves):
        core = 1 - c if p == 0 else c
        total = None
        for pieces, k in zip(bands, shifts):
            columns = pl.ds(pl.multiple_of(core * h, h), h)
            ranks = split(jnp.concatenate([p[:, columns] for p in pieces]).T)
            n = high_ref.shape[0] // 4
            rows = pl.ds(pl.multiple_of(lax.rem(y + 4 - k, 4) * n, n), n)
            term = dot3(ranks, (high_ref[rows], low_ref[rows]))
            total = term if total is None else total + term
        for i in range(4):
            for j in range(tiles):
                at = slice(i * block + j * own, i * block + (j + 1) * own)
                piece = total[i * own : (i + 1) * own, j * TILE : (j + 1) * TILE]
                half[at] = piece + before[p][at] if accumulate else piece
            at = slice(i * block + tiles * own, (i + 1) * block)
            piece = packed_ref[pl.ds(pl.multiple_of((core * 4 + i) * eighth, 8), eighth)]
            half[at] = piece + before[p][at] if accumulate else piece


def settle_kernel(*refs):
    terms, (crossed_ref, packed_ref) = refs[:-2], refs[-2:]
    total = terms[0][...]
    for a in terms[1:]:
        total = total + a[...]
    n = crossed_ref.shape[0]
    crossed_ref[...] = total[:n]
    packed_ref[...] = total[n:]


def unpack(packed_ref, gram_ref):
    at = 0
    for i in range(RANK // TILE):
        for j in range(i + 1):
            block = packed_ref[at : at + TILE]
            rows, columns = slice(i * TILE, (i + 1) * TILE), slice(j * TILE, (j + 1) * TILE)
            gram_ref[rows, columns] = block
            if i != j:
                gram_ref[columns, rows] = block.T
            at += TILE


def eliminate(gram_ref, inverse_ref):
    n = gram_ref.shape[0]
    row = lax.broadcasted_iota(jnp.int32, (n, n), 0)
    column = lax.broadcasted_iota(jnp.int32, (n, n), 1)
    inverse_ref[...] = (row == column).astype(jnp.float32)

    def step(j, _):
        gram, inverse = gram_ref[...], inverse_ref[...]
        below = lax.broadcasted_iota(jnp.int32, (n, 1), 0)
        pivot_row = jnp.sum(jnp.where(row == j, gram, 0.0), axis=0, keepdims=True)
        pivot_inverse = jnp.sum(jnp.where(row == j, inverse, 0.0), axis=0, keepdims=True)
        pivot = jnp.sum(jnp.where(column[:1] == j, pivot_row, 0.0), axis=1, keepdims=True)
        scale = 1.0 / jnp.sqrt(pivot)
        factor = jnp.sum(jnp.where(column == j, gram, 0.0), axis=1, keepdims=True) * scale
        factor = jnp.where(below > j, factor, 0.0)
        gram_ref[...] = gram - factor * (pivot_row * scale)
        inverse = inverse - factor * (pivot_inverse * scale)
        inverse_ref[...] = jnp.where(row == j, pivot_inverse * scale, inverse)
        return 0

    lax.fori_loop(0, n, step, 0)


def inverse_factor_kernel(order_ref, *refs):
    blocks, (inverse_ref, packed_ref, gram_ref, w_ref) = refs[:8], refs[8:]
    n, h = RANK, RANK // 2
    rows = blocks[0].shape[0]
    for i, block in enumerate(blocks):
        packed_ref[pl.ds(pl.multiple_of(order_ref[i] * rows, 8), rows)] = block[...]
    unpack(packed_ref, gram_ref)
    row = lax.broadcasted_iota(jnp.int32, (n, n), 0)
    column = lax.broadcasted_iota(jnp.int32, (n, n), 1)
    eye = (row == column).astype(jnp.float32)
    keep = jnp.where(row > column, 1.0, 0.5 * eye)
    gram = gram_ref[...]
    diagonal = gram * eye
    by_row = lax.rsqrt(jnp.sum(diagonal, axis=1, keepdims=True))
    by_column = lax.rsqrt(jnp.sum(diagonal, axis=0, keepdims=True))
    scaled = gram * by_row * by_column
    w_ref[...] = eye - (scaled - eye) * keep
    top, low = split(scaled)
    a11, a12, a21, a22 = (
        (top[r, c], low[r, c]) for r in (slice(0, h), slice(h, n)) for c in (slice(0, h), slice(h, n))
    )
    eye_h, keep_h = eye[:h, :h], keep[:h, :h]

    def more(state):
        step, residual = state
        return jnp.logical_and(step < MOST_STEPS, jnp.logical_not(residual < CLOSE))

    def update(state, product=dot3):
        step, _ = state
        w11, w21, w22 = split(w_ref[:h, :h]), split(w_ref[h:, :h]), split(w_ref[h:, h:])
        t11 = split(product(w11, a11))
        t21 = split(product(w21, a11) + product(w22, a21))
        t22 = split(product(w21, a12) + product(w22, a22))
        e11 = product(t11, w11, (1, 1)) - eye_h
        e21 = product(t21, w11, (1, 1))
        e22 = product(t21, w21, (1, 1)) + product(t22, w22, (1, 1)) - eye_h
        p11, p21, p22 = split(e11 * keep_h), split(e21), split(e22 * keep_h)
        w_ref[:h, :h] = w_ref[:h, :h] - dot1(p11, w11)
        w_ref[h:, :h] = w_ref[h:, :h] - (dot1(p21, w11) + dot1(p22, w21))
        w_ref[h:, h:] = w_ref[h:, h:] - dot1(p22, w22)
        return step + 1, jnp.sqrt(jnp.sum(e11 * e11) + 2.0 * jnp.sum(e21 * e21) + jnp.sum(e22 * e22))

    start = update((jnp.int32(0), None), dot1)
    _, residual = lax.while_loop(more, update, (start[0], jnp.float32(1.0)))
    inverse_ref[...] = w_ref[...] * by_column

    @pl.when(jnp.logical_not(residual < CLOSE))
    def _():
        eliminate(gram_ref, inverse_ref)


def orth_kernel(y_ref, inverse_ref, *refs):
    bands, out_ref = refs[:-1], refs[-1]
    inverse = split(inverse_ref[...])
    n = out_ref.shape[0] // 4
    for band, (k, first) in zip(bands, ((0, 0), (1, 0), (1, n // 2), (2, 0), (2, n // 2), (3, 0), (3, n // 2))):
        at = pl.ds(pl.multiple_of(lax.rem(y_ref[0] + 4 - k, 4) * n + first, TILE), band.shape[0])
        out_ref[at] = dot3(split(band[...]), inverse, (1, 1))


def right_kernel(order_ref, place_ref, *refs):
    blocks, (inverse_ref, high_ref, low_ref, own_ref, squared_ref, crossed_ref, right_ref) = refs[:8], refs[8:]
    rows, h = RANK // 8, RANK // 2
    tiles = high_ref.shape[1] // TILE
    for i, block in enumerate(blocks):
        at = pl.ds(pl.multiple_of(order_ref[i] * rows, rows), rows)
        for j in range(tiles):
            crossed_ref[at, j * TILE : (j + 1) * TILE] = block[j * rows : (j + 1) * rows]
    crossed = split(crossed_ref[...])
    inverse = split(inverse_ref[...])
    right_ref[:h] = dot3(tuple(p[:h, :h] for p in inverse), tuple(p[:h] for p in crossed))
    right_ref[h:] = dot3(tuple(p[h:] for p in inverse), crossed)
    right = right_ref[...]
    high_ref[...], low_ref[...] = split(right)
    own_ref[...] = right_ref[pl.ds(pl.multiple_of(place_ref[0] * rows, rows), rows)]
    total = right[:, :TILE] * right[:, :TILE]
    for j in range(1, tiles):
        piece = right[:, j * TILE : (j + 1) * TILE]
        total = total + piece * piece
    sums = jnp.sum(total.T, axis=0, keepdims=True)
    for i in range(RANK // TILE):
        squared_ref[:, i, :] = jnp.broadcast_to(sums[:, i * TILE : (i + 1) * TILE], (squared_ref.shape[0], TILE))


def momentum_kernel(momentum_ref, gradient_ref, orth_ref, right_ref, out_ref):
    product = jnp.dot(orth_ref[...].astype(jnp.bfloat16), right_ref[...], preferred_element_type=jnp.float32)
    out_ref[...] = (momentum_ref[...] + gradient_ref[...].astype(jnp.float32)) - decay_rest * product


def update_kernel(place_ref, squared_ref, own_ref, orth_ref, high_ref, low_ref, update_ref, factor_ref):
    squared = jnp.sum(squared_ref[...], axis=0)
    over = 1.0 / jnp.sqrt(squared + epsilon)
    over = jnp.concatenate([over[i : i + 1] for i in range(RANK // TILE)], axis=1)

    @pl.when(pl.program_id(0) == 0)
    def _():
        rows = factor_ref.shape[0]
        row = lax.broadcasted_iota(jnp.int32, (rows, RANK), 0)
        column = lax.broadcasted_iota(jnp.int32, (rows, RANK), 1)
        here = column == row + place_ref[0] * rows
        scale = jnp.sum(jnp.where(here, jnp.broadcast_to(over, (rows, RANK)), 0.0), axis=1, keepdims=True)
        factor_ref[...] = own_ref[...] * scale

    orth = split(orth_ref[...] * over)
    update_ref[...] = (math.sqrt(D * FF / RANK) * dot3(orth, (high_ref[...], low_ref[...]))).astype(jnp.bfloat16)


def in_hbm(a):
    return pltpu.with_memory_space_constraint(a, pltpu.HBM)


def in_vmem(a):
    return pltpu.with_memory_space_constraint(a, pltpu.VMEM)


VMEM_BYTES = 20 * 2**20
VMEM, SMEM = pl.BlockSpec(memory_space=pltpu.VMEM), pl.BlockSpec(memory_space=pltpu.SMEM)


def call(kernel, given, out, scratch=(), name=None):
    return pl.pallas_call(
        kernel,
        out_shape=out,
        in_specs=[SMEM if a.dtype == jnp.int32 else VMEM for a in given],
        out_specs=jax.tree.map(lambda _: VMEM, out),
        scratch_shapes=list(scratch),
        compiler_params=pltpu.CompilerParams(vmem_limit_bytes=VMEM_BYTES),
        cost_estimate=pl.CostEstimate(flops=1, bytes_accessed=1, transcendentals=0),
        name=name,
    )(*given)


def f32(*shape):
    return jax.ShapeDtypeStruct(shape, jnp.float32)


def by_rows(kernel, given, out, scratch=(), name=None, steps=4):
    n = D // 8

    def spec(a):
        if a.shape[0] == n:
            return pl.BlockSpec((n // steps, a.shape[1]), lambda i: (i, 0))
        if a.dtype == jnp.int32:
            return SMEM
        return pl.BlockSpec(a.shape, lambda i: (0,) * len(a.shape))

    return pl.pallas_call(
        kernel,
        grid=(steps,),
        out_shape=out,
        in_specs=[spec(a) for a in given],
        out_specs=jax.tree.map(spec, out),
        scratch_shapes=list(scratch),
        compiler_params=pltpu.CompilerParams(vmem_limit_bytes=VMEM_BYTES),
        cost_estimate=pl.CostEstimate(flops=1, bytes_accessed=1, transcendentals=0),
        name=name,
    )(*given)


def per_device(momentum, gradient, right_factor):
    x, c, y = lax.axis_index("x"), lax.axis_index("c"), lax.axis_index("y")
    rows, columns = momentum.shape[0] // SIZES["y"], momentum.shape[1]
    wide = jax.ShapeDtypeStruct(momentum.shape, jnp.bfloat16)
    combined = by_rows(combine_kernel, (momentum, gradient), (wide, wide), name="combine")

    factor = relative(right_factor, "x")
    factor, combined = lax.optimization_barrier((factor, combined))
    factor = factor + [shift(b, "c", 1) for b in factor]
    order = jnp.stack([((x - k) % 4) * 2 + p for p in (c, 1 - c) for k in range(4)])
    terms = call(
        left_kernel,
        (order, y[None], *factor, combined[0], in_hbm(combined[1])),
        [f32(rows // 2, RANK)] * 8,
        [pltpu.VMEM((RANK, columns), jnp.float32), pltpu.VMEM((4 * rows, RANK), jnp.float32)],
        "left",
    )
    by_next, by_last = shift(terms[4], "y", 1), shift(terms[5], "y", 3)
    plain = shift(terms[3], "y", 1), shift(terms[6], "y", 3)
    passed = shift(terms[2] + by_next, "y", 1), shift(terms[7] + by_last, "y", 3)
    band = call(
        join_kernel, (terms[0], passed[0], plain[1], terms[1], plain[0], passed[1]), f32(rows, RANK), name="join"
    )
    band = summed_z(band)
    top, bottom = band[: rows // 2], band[rows // 2 :]
    ahead_top, behind_bottom = shift(top, "y", 3), shift(bottom, "y", 1)
    behind = shift(top, "y", 1), behind_bottom
    ahead = ahead_top, shift(bottom, "y", 3)
    across = shift(ahead_top, "y", 3), shift(behind_bottom, "y", 1)

    place = jnp.stack([c, y])
    own, eighth = RANK // 8 * (columns // TILE), 10 * TILE // 8
    block = own + eighth
    halves = None
    for name, shifts, pieces in (("own", (0,), (band,)), ("near", (1, 3), behind + ahead), ("far", (2,), across)):
        halves = call(
            functools.partial(absorb_kernel, shifts, halves is not None),
            (place, *pieces, *map(in_vmem, combined), *(halves or ())),
            (f32(4 * block, TILE), f32(4 * block, TILE)),
            [pltpu.VMEM((10 * TILE, TILE), jnp.float32)],
            "absorb_" + name,
        )
    sent, kept = halves
    came = shift(sent, "c", 1)
    parts = [block_of(came, (x + k) % 4, block) + block_of(kept, (x + k) % 4, block) for k in range(4)]
    terms = [parts[0]] + [shift(parts[k], "x", k) for k in range(1, 4)]
    crossed, packed = call(settle_kernel, terms, (f32(own, TILE), f32(eighth, TILE)), name="settle")
    packed = relative(packed, "x")
    near = shift(crossed, "x", 1), shift(crossed, "x", 3)
    far, packed = lax.optimization_barrier((crossed, packed))
    crossed = [crossed, near[0], shift(far, "x", 2), near[1]]
    packed = packed + [shift(b, "c", 1) for b in packed]
    order = jnp.stack([p * 4 + (x - k) % 4 for p in (c, 1 - c) for k in range(4)])
    inverse = call(
        inverse_factor_kernel,
        (order, *packed),
        f32(RANK, RANK),
        [pltpu.VMEM((10 * TILE, TILE), jnp.float32)] + [pltpu.VMEM((RANK, RANK), jnp.float32)] * 2,
        name="inverse_factor",
    )
    orth = call(orth_kernel, (y[None], inverse, *map(in_hbm, (band, *behind, *across, *ahead))), f32(momentum.shape[0], RANK), name="orth")
    crossed, orth = lax.optimization_barrier((crossed, orth))
    crossed = crossed + [shift(b, "c", 1) for b in crossed]
    place = (x * 2 + c)[None]
    half_width = jax.ShapeDtypeStruct((RANK, columns), jnp.bfloat16)
    high, low, right, squared = call(
        right_kernel,
        (order, place, *map(in_hbm, crossed), inverse),
        (half_width, half_width, f32(*right_factor.shape), f32(32, RANK // TILE, TILE)),
        [pltpu.VMEM((RANK, columns), jnp.float32)] * 2,
        "right",
    )
    squared = exchange(squared, COLS)
    new_momentum = by_rows(
        momentum_kernel, (in_hbm(momentum), in_hbm(gradient), orth, in_hbm(high)), f32(*momentum.shape), name="momentum"
    )
    squared, new_momentum = lax.optimization_barrier((squared, new_momentum))
    update, new_factor = by_rows(
        update_kernel,
        (place, squared, right, orth, in_hbm(high), in_hbm(low)),
        (wide, f32(*right_factor.shape)),
        name="update",
        steps=2,
    )
    return (new_momentum, update, new_factor)


def solution(mesh):
    split_mesh = Mesh(mesh.devices.reshape(tuple(SIZES.values())), tuple(SIZES))
    spec = P(ROWS, COLS)
    return jax.shard_map(
        per_device, mesh=split_mesh, in_specs=(spec, spec, spec), out_specs=(spec, spec, spec), check_vma=False
    )
```

```python
import functools
import math

import jax
import jax.numpy as jnp
from jax import lax
from jax.experimental import pallas as pl
from jax.experimental.pallas import tpu as pltpu
from jax.sharding import Mesh
from jax.sharding import PartitionSpec as P

D = 8192
FF = 28672
RANK = 512

decay_rest = 0.05
epsilon = 1e-06

SIZES = {"x": 4, "c": 2, "y": 4, "z": 8}
ROWS = ("x", "c")
COLS = ("y", "z")

CLOSE = 5e-3
MOST_STEPS = 9

TILE = 128


def shift(a, axis, k):
    n = SIZES[axis]
    return lax.ppermute(a, axis, [(i, (i + k) % n) for i in range(n)])


def block_of(a, index, rows):
    return lax.dynamic_slice_in_dim(a, index * rows, rows, 0)


def summed_z(a):
    spread = call(spread_kernel, (exchange(a, "z"),), f32(*a.shape), [], name="spread")
    return exchange(spread, "z")


def exchange(a, axes):
    return lax.all_to_all(a, axes, split_axis=0, concat_axis=0, tiled=True)


def relative(a, axis):
    return [a] + [shift(a, axis, k) for k in range(1, SIZES[axis])]


def split(a):
    high = a.astype(jnp.bfloat16)
    return high, (a - high.astype(jnp.float32)).astype(jnp.bfloat16)


def dot3(a, b, contract=(1, 0)):
    (ah, al), (bh, bl) = a, b
    dims = (((contract[0],), (contract[1],)), ((), ()))
    n = ah.shape[0]
    both = lax.dot_general(jnp.concatenate([ah, al]), bh, dims, preferred_element_type=jnp.float32)
    return both[:n] + (both[n:] + lax.dot_general(ah, bl, dims, preferred_element_type=jnp.float32))


def dot1(a, b, contract=(1, 0)):
    return lax.dot_general(
        a[0], b[0], (((contract[0],), (contract[1],)), ((), ())), preferred_element_type=jnp.float32
    )


def spread_kernel(parts_ref, out_ref):
    rows = parts_ref.shape[0] // SIZES["z"]
    total = parts_ref[:rows]
    for i in range(1, SIZES["z"]):
        total = total + parts_ref[i * rows : (i + 1) * rows]
    for i in range(SIZES["z"]):
        out_ref[i * rows : (i + 1) * rows] = total


def join_kernel(*refs):
    parts, out_ref = refs[:-1], refs[-1]
    n = parts[0].shape[0]
    out_ref[:n] = parts[0][...] + parts[1][...] + parts[2][...]
    out_ref[n:] = parts[3][...] + parts[4][...] + parts[5][...]


def combine_kernel(momentum_ref, gradient_ref, high_ref, low_ref):
    high_ref[...], low_ref[...] = split(momentum_ref[...] + gradient_ref[...].astype(jnp.float32))


def left_kernel(order_ref, y_ref, *refs):
    blocks, (high_ref, low_ref), outs, (factor_ref, left_ref) = refs[:8], refs[8:10], refs[10:18], refs[18:]
    rows = blocks[0].shape[0]
    for i, block in enumerate(blocks):
        factor_ref[pl.ds(pl.multiple_of(order_ref[i] * rows, rows), rows)] = block[...]
    factor = split(factor_ref[...].T)
    n = outs[0].shape[0]
    for i in range(4):
        at = slice(2 * i * n, 2 * (i + 1) * n)
        left_ref[at] = dot3((high_ref[at], low_ref[at]), factor)
    for k, out in enumerate(outs):
        out[...] = left_ref[pl.ds(pl.multiple_of(lax.rem(2 * y_ref[0] + k, 8) * n, n), n)]


def absorb_kernel(shifts, accumulate, place_ref, *refs):
    bands = []
    for k in shifts:
        n = 2 if k else 1
        bands, refs = bands + [refs[:n]], refs[n:]
    (high_ref, low_ref), refs = refs[:2], refs[2:]
    before, refs = (refs[:2], refs[2:]) if accumulate else (None, refs)
    halves, (packed_ref,) = refs[:2], refs[2:]
    c, y = place_ref[0], place_ref[1]
    h, own, eighth = RANK // 2, RANK // 8, packed_ref.shape[0] // 8
    tiles = high_ref.shape[1] // TILE
    block = halves[0].shape[0] // 4
    grams = [None] * (RANK // TILE)
    for pieces in bands:
        band = jnp.concatenate([p[...] for p in pieces])
        across, down = split(band.T), split(band)
        for i in range(RANK // TILE):
            product = dot3(
                tuple(p[i * TILE : (i + 1) * TILE] for p in across), tuple(p[:, : (i + 1) * TILE] for p in down)
            )
            grams[i] = product if grams[i] is None else grams[i] + product
    at = 0
    for i, product in enumerate(grams):
        for j in range(i + 1):
            packed_ref[at : at + TILE] = product[:, j * TILE : (j + 1) * TILE]
            at += TILE
    for p, half in enumerate(halves):
        core = 1 - c if p == 0 else c
        total = None
        for pieces, k in zip(bands, shifts):
            columns = pl.ds(pl.multiple_of(core * h, h), h)
            ranks = split(jnp.concatenate([p[:, columns] for p in pieces]).T)
            n = high_ref.shape[0] // 4
            rows = pl.ds(pl.multiple_of(lax.rem(y + 4 - k, 4) * n, n), n)
            term = dot3(ranks, (high_ref[rows], low_ref[rows]))
            total = term if total is None else total + term
        for i in range(4):
            for j in range(tiles):
                at = slice(i * block + j * own, i * block + (j + 1) * own)
                piece = total[i * own : (i + 1) * own, j * TILE : (j + 1) * TILE]
                half[at] = piece + before[p][at] if accumulate else piece
            at = slice(i * block + tiles * own, (i + 1) * block)
            piece = packed_ref[pl.ds(pl.multiple_of((core * 4 + i) * eighth, 8), eighth)]
            half[at] = piece + before[p][at] if accumulate else piece


def settle_kernel(*refs):
    terms, (crossed_ref, packed_ref) = refs[:-2], refs[-2:]
    total = terms[0][...]
    for a in terms[1:]:
        total = total + a[...]
    n = crossed_ref.shape[0]
    crossed_ref[...] = total[:n]
    packed_ref[...] = total[n:]


def unpack(packed_ref, gram_ref):
    at = 0
    for i in range(RANK // TILE):
        for j in range(i + 1):
            block = packed_ref[at : at + TILE]
            rows, columns = slice(i * TILE, (i + 1) * TILE), slice(j * TILE, (j + 1) * TILE)
            gram_ref[rows, columns] = block
            if i != j:
                gram_ref[columns, rows] = block.T
            at += TILE


def eliminate(gram_ref, inverse_ref):
    n = gram_ref.shape[0]
    row = lax.broadcasted_iota(jnp.int32, (n, n), 0)
    column = lax.broadcasted_iota(jnp.int32, (n, n), 1)
    inverse_ref[...] = (row == column).astype(jnp.float32)

    def step(j, _):
        gram, inverse = gram_ref[...], inverse_ref[...]
        below = lax.broadcasted_iota(jnp.int32, (n, 1), 0)
        pivot_row = jnp.sum(jnp.where(row == j, gram, 0.0), axis=0, keepdims=True)
        pivot_inverse = jnp.sum(jnp.where(row == j, inverse, 0.0), axis=0, keepdims=True)
        pivot = jnp.sum(jnp.where(column[:1] == j, pivot_row, 0.0), axis=1, keepdims=True)
        scale = 1.0 / jnp.sqrt(pivot)
        factor = jnp.sum(jnp.where(column == j, gram, 0.0), axis=1, keepdims=True) * scale
        factor = jnp.where(below > j, factor, 0.0)
        gram_ref[...] = gram - factor * (pivot_row * scale)
        inverse = inverse - factor * (pivot_inverse * scale)
        inverse_ref[...] = jnp.where(row == j, pivot_inverse * scale, inverse)
        return 0

    lax.fori_loop(0, n, step, 0)


def inverse_factor_kernel(order_ref, *refs):
    blocks, (inverse_ref, packed_ref, gram_ref, w_ref) = refs[:8], refs[8:]
    n, h = RANK, RANK // 2
    rows = blocks[0].shape[0]
    for i, block in enumerate(blocks):
        packed_ref[pl.ds(pl.multiple_of(order_ref[i] * rows, 8), rows)] = block[...]
    unpack(packed_ref, gram_ref)
    row = lax.broadcasted_iota(jnp.int32, (n, n), 0)
    column = lax.broadcasted_iota(jnp.int32, (n, n), 1)
    eye = (row == column).astype(jnp.float32)
    keep = jnp.where(row > column, 1.0, 0.5 * eye)
    gram = gram_ref[...]
    diagonal = gram * eye
    by_row = lax.rsqrt(jnp.sum(diagonal, axis=1, keepdims=True))
    by_column = lax.rsqrt(jnp.sum(diagonal, axis=0, keepdims=True))
    scaled = gram * by_row * by_column
    w_ref[...] = eye - (scaled - eye) * keep
    top, low = split(scaled)
    a11, a12, a21, a22 = (
        (top[r, c], low[r, c]) for r in (slice(0, h), slice(h, n)) for c in (slice(0, h), slice(h, n))
    )
    eye_h, keep_h = eye[:h, :h], keep[:h, :h]

    def more(state):
        step, residual = state
        return jnp.logical_and(step < MOST_STEPS, jnp.logical_not(residual < CLOSE))

    def update(state, product=dot3):
        step, _ = state
        w11, w21, w22 = split(w_ref[:h, :h]), split(w_ref[h:, :h]), split(w_ref[h:, h:])
        t11 = split(product(w11, a11))
        t21 = split(product(w21, a11) + product(w22, a21))
        t22 = split(product(w21, a12) + product(w22, a22))
        e11 = product(t11, w11, (1, 1)) - eye_h
        e21 = product(t21, w11, (1, 1))
        e22 = product(t21, w21, (1, 1)) + product(t22, w22, (1, 1)) - eye_h
        p11, p21, p22 = split(e11 * keep_h), split(e21), split(e22 * keep_h)
        w_ref[:h, :h] = w_ref[:h, :h] - dot1(p11, w11)
        w_ref[h:, :h] = w_ref[h:, :h] - (dot1(p21, w11) + dot1(p22, w21))
        w_ref[h:, h:] = w_ref[h:, h:] - dot1(p22, w22)
        return step + 1, jnp.sqrt(jnp.sum(e11 * e11) + 2.0 * jnp.sum(e21 * e21) + jnp.sum(e22 * e22))

    start = update((jnp.int32(0), None), dot1)
    _, residual = lax.while_loop(more, update, (start[0], jnp.float32(1.0)))
    inverse_ref[...] = w_ref[...] * by_column

    @pl.when(jnp.logical_not(residual < CLOSE))
    def _():
        eliminate(gram_ref, inverse_ref)


def orth_kernel(y_ref, inverse_ref, *refs):
    bands, out_ref = refs[:-1], refs[-1]
    inverse = split(inverse_ref[...])
    n = out_ref.shape[0] // 4
    for band, (k, first) in zip(bands, ((0, 0), (1, 0), (1, n // 2), (2, 0), (2, n // 2), (3, 0), (3, n // 2))):
        at = pl.ds(pl.multiple_of(lax.rem(y_ref[0] + 4 - k, 4) * n + first, TILE), band.shape[0])
        out_ref[at] = dot3(split(band[...]), inverse, (1, 1))


def right_kernel(order_ref, place_ref, *refs):
    blocks, (inverse_ref, high_ref, low_ref, own_ref, squared_ref, crossed_ref, right_ref) = refs[:8], refs[8:]
    rows, h = RANK // 8, RANK // 2
    tiles = high_ref.shape[1] // TILE
    for i, block in enumerate(blocks):
        at = pl.ds(pl.multiple_of(order_ref[i] * rows, rows), rows)
        for j in range(tiles):
            crossed_ref[at, j * TILE : (j + 1) * TILE] = block[j * rows : (j + 1) * rows]
    crossed = split(crossed_ref[...])
    inverse = split(inverse_ref[...])
    right_ref[:h] = dot3(tuple(p[:h, :h] for p in inverse), tuple(p[:h] for p in crossed))
    right_ref[h:] = dot3(tuple(p[h:] for p in inverse), crossed)
    right = right_ref[...]
    high_ref[...], low_ref[...] = split(right)
    own_ref[...] = right_ref[pl.ds(pl.multiple_of(place_ref[0] * rows, rows), rows)]
    total = right[:, :TILE] * right[:, :TILE]
    for j in range(1, tiles):
        piece = right[:, j * TILE : (j + 1) * TILE]
        total = total + piece * piece
    sums = jnp.sum(total.T, axis=0, keepdims=True)
    for i in range(RANK // TILE):
        squared_ref[:, i, :] = jnp.broadcast_to(sums[:, i * TILE : (i + 1) * TILE], (squared_ref.shape[0], TILE))


def momentum_kernel(momentum_ref, gradient_ref, orth_ref, high_ref, low_ref, out_ref, high_out, low_out):
    @pl.when(pl.program_id(0) == 0)
    def _():
        high_out[...], low_out[...] = high_ref[...], low_ref[...]

    product = jnp.dot(orth_ref[...].astype(jnp.bfloat16), high_ref[...], preferred_element_type=jnp.float32)
    out_ref[...] = (momentum_ref[...] + gradient_ref[...].astype(jnp.float32)) - decay_rest * product


def update_kernel(place_ref, squared_ref, own_ref, orth_ref, high_ref, low_ref, update_ref, factor_ref):
    squared = jnp.sum(squared_ref[...], axis=0)
    over = 1.0 / jnp.sqrt(squared + epsilon)
    over = jnp.concatenate([over[i : i + 1] for i in range(RANK // TILE)], axis=1)

    @pl.when(pl.program_id(0) == 0)
    def _():
        rows = factor_ref.shape[0]
        row = lax.broadcasted_iota(jnp.int32, (rows, RANK), 0)
        column = lax.broadcasted_iota(jnp.int32, (rows, RANK), 1)
        here = column == row + place_ref[0] * rows
        scale = jnp.sum(jnp.where(here, jnp.broadcast_to(over, (rows, RANK)), 0.0), axis=1, keepdims=True)
        factor_ref[...] = own_ref[...] * scale

    orth = split(orth_ref[...] * over)
    update_ref[...] = (math.sqrt(D * FF / RANK) * dot3(orth, (high_ref[...], low_ref[...]))).astype(jnp.bfloat16)


def in_hbm(a):
    return pltpu.with_memory_space_constraint(a, pltpu.HBM)


def in_vmem(a):
    return pltpu.with_memory_space_constraint(a, pltpu.VMEM)


VMEM_BYTES = 20 * 2**20
VMEM, SMEM = pl.BlockSpec(memory_space=pltpu.VMEM), pl.BlockSpec(memory_space=pltpu.SMEM)


def call(kernel, given, out, scratch=(), name=None):
    return pl.pallas_call(
        kernel,
        out_shape=out,
        in_specs=[SMEM if a.dtype == jnp.int32 else VMEM for a in given],
        out_specs=jax.tree.map(lambda _: VMEM, out),
        scratch_shapes=list(scratch),
        compiler_params=pltpu.CompilerParams(vmem_limit_bytes=VMEM_BYTES),
        cost_estimate=pl.CostEstimate(flops=1, bytes_accessed=1, transcendentals=0),
        name=name,
    )(*given)


def f32(*shape):
    return jax.ShapeDtypeStruct(shape, jnp.float32)


def by_rows(kernel, given, out, scratch=(), name=None, steps=4):
    n = D // 8

    def spec(a):
        if a.shape[0] == n:
            return pl.BlockSpec((n // steps, a.shape[1]), lambda i: (i, 0))
        if a.dtype == jnp.int32:
            return SMEM
        return pl.BlockSpec(a.shape, lambda i: (0,) * len(a.shape))

    return pl.pallas_call(
        kernel,
        grid=(steps,),
        out_shape=out,
        in_specs=[spec(a) for a in given],
        out_specs=jax.tree.map(spec, out),
        scratch_shapes=list(scratch),
        compiler_params=pltpu.CompilerParams(vmem_limit_bytes=32 * 2**20),
        cost_estimate=pl.CostEstimate(flops=1, bytes_accessed=1, transcendentals=0),
        name=name,
    )(*given)


def per_device(momentum, gradient, right_factor):
    x, c, y = lax.axis_index("x"), lax.axis_index("c"), lax.axis_index("y")
    rows, columns = momentum.shape[0] // SIZES["y"], momentum.shape[1]
    wide = jax.ShapeDtypeStruct(momentum.shape, jnp.bfloat16)
    combined = by_rows(combine_kernel, (momentum, gradient), (wide, wide), name="combine")

    factor = relative(right_factor, "x")
    factor, combined = lax.optimization_barrier((factor, combined))
    factor = factor + [shift(b, "c", 1) for b in factor]
    order = jnp.stack([((x - k) % 4) * 2 + p for p in (c, 1 - c) for k in range(4)])
    terms = call(
        left_kernel,
        (order, y[None], *factor, combined[0], in_hbm(combined[1])),
        [f32(rows // 2, RANK)] * 8,
        [pltpu.VMEM((RANK, columns), jnp.float32), pltpu.VMEM((4 * rows, RANK), jnp.float32)],
        "left",
    )
    by_next, by_last = shift(terms[4], "y", 1), shift(terms[5], "y", 3)
    plain = shift(terms[3], "y", 1), shift(terms[6], "y", 3)
    passed = shift(terms[2] + by_next, "y", 1), shift(terms[7] + by_last, "y", 3)
    band = call(
        join_kernel, (terms[0], passed[0], plain[1], terms[1], plain[0], passed[1]), f32(rows, RANK), name="join"
    )
    band = summed_z(band)
    top, bottom = band[: rows // 2], band[rows // 2 :]
    ahead_top, behind_bottom = shift(top, "y", 3), shift(bottom, "y", 1)
    behind = shift(top, "y", 1), behind_bottom
    ahead = ahead_top, shift(bottom, "y", 3)
    across = shift(ahead_top, "y", 3), shift(behind_bottom, "y", 1)

    place = jnp.stack([c, y])
    own, eighth = RANK // 8 * (columns // TILE), 10 * TILE // 8
    block = own + eighth
    halves = None
    for name, shifts, pieces in (("own", (0,), (band,)), ("near", (1, 3), behind + ahead), ("far", (2,), across)):
        halves = call(
            functools.partial(absorb_kernel, shifts, halves is not None),
            (place, *pieces, *map(in_vmem, combined), *(halves or ())),
            (f32(4 * block, TILE), f32(4 * block, TILE)),
            [pltpu.VMEM((10 * TILE, TILE), jnp.float32)],
            "absorb_" + name,
        )
    sent, kept = halves
    came = shift(sent, "c", 1)
    parts = [block_of(came, (x + k) % 4, block) + block_of(kept, (x + k) % 4, block) for k in range(4)]
    terms = [parts[0]] + [shift(parts[k], "x", k) for k in range(1, 4)]
    crossed, packed = call(settle_kernel, terms, (f32(own, TILE), f32(eighth, TILE)), name="settle")
    packed = relative(packed, "x")
    near = shift(crossed, "x", 1), shift(crossed, "x", 3)
    far, packed = lax.optimization_barrier((crossed, packed))
    crossed = [crossed, near[0], shift(far, "x", 2), near[1]]
    packed = packed + [shift(b, "c", 1) for b in packed]
    order = jnp.stack([p * 4 + (x - k) % 4 for p in (c, 1 - c) for k in range(4)])
    inverse = call(
        inverse_factor_kernel,
        (order, *packed),
        f32(RANK, RANK),
        [pltpu.VMEM((10 * TILE, TILE), jnp.float32)] + [pltpu.VMEM((RANK, RANK), jnp.float32)] * 2,
        name="inverse_factor",
    )
    orth = call(orth_kernel, (y[None], inverse, *map(in_hbm, (band, *behind, *across, *ahead))), f32(momentum.shape[0], RANK), name="orth")
    crossed, orth = lax.optimization_barrier((crossed, orth))
    crossed = crossed + [shift(b, "c", 1) for b in crossed]
    place = (x * 2 + c)[None]
    half_width = jax.ShapeDtypeStruct((RANK, columns), jnp.bfloat16)
    high, low, right, squared = call(
        right_kernel,
        (order, place, *map(in_hbm, crossed), inverse),
        (half_width, half_width, f32(*right_factor.shape), f32(32, RANK // TILE, TILE)),
        [pltpu.VMEM((RANK, columns), jnp.float32)] * 2,
        "right",
    )
    squared = exchange(squared, COLS)
    new_momentum, high, low = by_rows(
        momentum_kernel,
        (in_hbm(momentum), in_hbm(gradient), orth, in_hbm(high), in_hbm(low)),
        (f32(*momentum.shape), half_width, half_width),
        name="momentum",
        steps=2,
    )
    squared, new_momentum = lax.optimization_barrier((squared, new_momentum))
    update, new_factor = by_rows(
        update_kernel,
        (place, squared, right, orth, high, low),
        (wide, f32(*right_factor.shape)),
        name="update",
        steps=2,
    )
    return (new_momentum, update, new_factor)


def solution(mesh):
    split_mesh = Mesh(mesh.devices.reshape(tuple(SIZES.values())), tuple(SIZES))
    spec = P(ROWS, COLS)
    return jax.shard_map(
        per_device, mesh=split_mesh, in_specs=(spec, spec, spec), out_specs=(spec, spec, spec), check_vma=False
    )
```
